32 devices in a mesh: grp: 8 (over y, x, core), tp: 4 (over z).
Axes of the slice: x: 2, y: 2, z: 4, core: 2. Of those that a mesh axis runs over, the one named last changes fastest.
Arguments:
- tokens: bfloat16 [4096, 8192], P('grp', 'tp'), may hold values from -6 to 6
- base_weight: bfloat16 [8192, 2048], P('tp'), may hold values from -0.0625 to 0.0625
- down_tables: bfloat16 [1024, 8192, 16], P('grp', 'tp'), may hold values from -0.0625 to 0.0625
- up_tables: bfloat16 [1024, 16, 2048], P('grp', None, 'tp'), may hold values from -1.5 to 1.5
- block_owner: int32 [32, 1], P('grp'), may hold values from 0 to 7; in each aligned block of 4 rows (0 to 3, 4 to 7, ...) at most 2 rows name the same one
- block_local: int32 [32], P('grp'), may hold values from 0 to 127
- block_count: int32 [32], P('grp'), may hold values from 1 to 128
Outputs:
- projected: bfloat16 [4096, 2048], P('grp', 'tp')
The draws below stay inside these ranges and needn't reach their ends.
Inputs may be any that keep to these rules, and one draw needn't show every extreme that they name: `block_owner`: among the 4 blocks of one group (an aligned run of 4 entries) no owner is named more than 2 times, a bound that some block reaches.
All inputs are finite; a program needn't handle non-finite values.
Results may differ from the reference program's by a relative error of at most 0.001.
Values may be sent and summed in bfloat16 or wider, within the bound.
No kernel may reach another device: no remote copies, remote signals or barrier semaphores. Data moves between devices by JAX's collectives and lax.ppermute only.
A program may use at most 64 MiB of HBM per device.

```python
import math
import jax
import jax.numpy as jnp
import numpy as np
from jax import lax

D = 8192
KEY_VALUE_COLUMNS = 2048
R = 16
BLOCK = 128
CAP = 2
ADP_GRP = 128
BLK_GRP = 4
GROUP_TOKEN_ROWS = 512
ROWS = 4096
BLOCKS = 32
ADP = 1024
N_GRP = 8


def with_ends(drawn, own_key, low, top_value):
    spot = [jax.random.randint(jax.random.fold_in(own_key, axis), (), 0, length) for axis, length in enumerate(drawn.shape)]
    main_axis = drawn.shape.index(max(drawn.shape))
    neighbour = spot[:main_axis] + [(spot[main_axis] + 1) % drawn.shape[main_axis]] + spot[main_axis + 1:]
    return drawn.at[tuple(spot)].set(low).at[tuple(neighbour)].set(top_value)


def steps_of(rng, dims, cuts, least, top_value):
    def one(position, shards_of):
        steps = jax.random.uniform(jax.random.fold_in(jax.random.fold_in(rng, 6), position), (shards_of,), jnp.float32, least / len(cuts), top_value / len(cuts))
        return jnp.repeat(jnp.exp(steps), dims[position] // shards_of).reshape((-1,) + (1,) * (len(dims) - position - 1))

    loudness = one(*cuts[0])
    for cut in cuts[1:]:
        loudness = loudness * one(*cut)
    return loudness


def assign_block(rng, own, number, rows, count, top, limit, skew):
    sequence = jax.random.permutation(rng, count)
    packed, usual = shares(count, rows * top, limit, skew, True), shares(count, rows * top, limit, skew, False)
    places = jnp.arange(count)

    def named(tallies, turn):
        used = int((tallies > 0).sum())
        fixed = max(1, used // 4)
        passed = fixed + (places - fixed + turn * (used - fixed)) % max(1, count - fixed)
        return jnp.zeros((count,), jnp.int32).at[sequence[jnp.where(places < fixed, places, passed)]].set(jnp.asarray(tallies, jnp.int32))

    tallies = jnp.where(number % 4 == 0, named(packed, number // 4), named(usual, number - number // 4 - 1))
    mixed = jax.random.permutation(jax.random.fold_in(own, 3), count)
    donor, taker = mixed[0:count // 2 * 2:2], mixed[1:count // 2 * 2:2]
    margin = jnp.minimum(tallies[donor] - 1, limit - tallies[taker]) // 2
    margin = jnp.where((donor == sequence[0]) | (taker == sequence[0]) | (tallies[taker] == 0), 0, jnp.maximum(margin, 0))
    passed = jax.random.randint(jax.random.fold_in(own, 4), (count // 2,), 0, 1 << 20) % (margin + 1)
    tallies = tallies.at[donor].add(-passed).at[taker].add(passed)
    labels = jnp.searchsorted(jnp.cumsum(tallies), jnp.arange(rows * top), side="right").astype(jnp.int32)
    table = labels.reshape(top, rows).T
    table = table[jax.random.permutation(jax.random.fold_in(own, 1), rows)]
    turn = jax.random.randint(jax.random.fold_in(own, 2), (rows, 1), 0, top)
    return jnp.take_along_axis(table, (jnp.arange(top)[None, :] + turn) % top, axis=1)


def shares(amount, total, limit, lean, full):
    portions = [(1 << 20) // math.isqrt(rank ** lean) + 1 for rank in range(1, amount + 1)]
    largest = limit if full else min(limit, max(-(-total // amount), total * portions[0] // sum(portions)))
    least = 1 if total - largest >= amount - 1 else 0
    holding, surplus = [largest] + [least] * (amount - 1), total - largest - least * (amount - 1)
    while surplus > 0:
        free = [i for i in range(1, amount) if holding[i] < largest] or [i for i in range(1, amount) if holding[i] < limit]
        pool, remaining = sum([portions[i] for i in free]), surplus
        for i in free:
            extra = min(limit - holding[i], max(1, remaining * portions[i] // pool), surplus)
            holding[i] = holding[i] + extra
            surplus = surplus - extra
    return np.array(holding)


def centred(stream_key, extent, deviation, bound, shards=(), held_as=jnp.bfloat16):
    values = deviation * jax.random.normal(stream_key, extent, jnp.float32)
    if shards:
        values = values * steps_of(stream_key, extent, shards, -0.22, 0.18)
    return jnp.clip(values, -bound, bound).astype(held_as)


def setup_inputs(seed: int = 0) -> dict:
    streams_of = jax.random.split(jax.random.key(seed), 8)
    tokens = centred(streams_of[0], (ROWS, D), 1.0, 6.0, ((0, 8), (1, 4)))
    base_weight = centred(streams_of[1], (D, KEY_VALUE_COLUMNS), D ** -0.5, 0.0625, ((0, 4),))
    down_tables = centred(streams_of[2], (ADP, D, R), D ** -0.5, 0.0625, ((0, 8), (1, 4)))
    up_tables = centred(streams_of[3], (ADP, R, KEY_VALUE_COLUMNS), R ** -0.5, 1.5, ((0, 8), (2, 4)))
    block_owner_keys = jax.random.split(jax.random.fold_in(streams_of[4], 1), BLOCKS // BLK_GRP)
    block_owner_turns = jax.random.permutation(jax.random.fold_in(streams_of[4], 3), BLOCKS // BLK_GRP)
    block_owner = jax.vmap(lambda own, number: assign_block(jax.random.fold_in(streams_of[4], 2), own, number, BLK_GRP, N_GRP, 1, CAP, 2))(block_owner_keys, block_owner_turns).reshape((BLOCKS, 1))
    block_local = with_ends(jax.random.randint(streams_of[5], (BLOCKS,), 0, ADP_GRP), jax.random.fold_in(streams_of[5], 1), 0, ADP_GRP - 1).astype(jnp.int32)
    block_count = with_ends(jax.random.randint(streams_of[6], (BLOCKS,), 1, BLOCK + 1), jax.random.fold_in(streams_of[6], 1), 1, BLOCK).astype(jnp.int32)
    return dict(tokens=tokens, base_weight=base_weight, down_tables=down_tables, up_tables=up_tables, block_owner=block_owner, block_local=block_local, block_count=block_count)


adapter_scale = 2.0


def reference(tokens, base_weight, down_tables, up_tables, block_owner, block_local, block_count):
    adapter = (block_owner[:, 0] * ADP_GRP + block_local).astype(jnp.int32)
    weight_full = base_weight.astype(jnp.float32)

    def one_group(group):
        first_row = (group * GROUP_TOKEN_ROWS).astype(jnp.int32)
        first_block = (group * BLK_GRP).astype(jnp.int32)
        group_rows = lax.dynamic_slice_in_dim(tokens, first_row, GROUP_TOKEN_ROWS, 0).astype(jnp.float32)
        group_ids = lax.dynamic_slice_in_dim(adapter, first_block, BLK_GRP, 0)
        group_count = lax.dynamic_slice_in_dim(block_count, first_block, BLK_GRP, 0)
        base_projection = jnp.dot(group_rows, weight_full, preferred_element_type=jnp.float32)
        down_sel = jnp.take(down_tables, group_ids, axis=0).astype(jnp.float32)
        up_sel = jnp.take(up_tables, group_ids, axis=0).astype(jnp.float32)
        blocked = group_rows.reshape(BLK_GRP, BLOCK, D)
        reduced = jnp.einsum('nbd,ndr->nbr', blocked, down_sel)
        rank_reduced_state = jnp.einsum('nbr,nro->nbo', reduced, up_sel, precision=lax.Precision.HIGHEST)
        projection_total = base_projection + adapter_scale * rank_reduced_state.reshape(GROUP_TOKEN_ROWS, KEY_VALUE_COLUMNS)
        offsets = jnp.arange(BLOCK, dtype=jnp.int32)
        live_rows = (offsets[None, :] < group_count[:, None]).reshape(GROUP_TOKEN_ROWS, 1)
        return jnp.where(live_rows, projection_total, jnp.float32(0.0)).astype(jnp.bfloat16)

    stacked = lax.map(one_group, jnp.arange(N_GRP, dtype=jnp.int32))
    return stacked.reshape(ROWS, KEY_VALUE_COLUMNS)
```

```python
import functools

import jax
import jax.numpy as jnp
from jax import lax
from jax.experimental import pallas as pl
from jax.experimental.pallas import tpu as pltpu
from jax.sharding import PartitionSpec as P

BLOCK = 128
CAP = 2
adapter_scale = 2.0
SEND_SCALE = 16.0
HBM = pl.BlockSpec(memory_space=pl.ANY)


def pack_kernel(group_count, ids_ref, me_ref, down_ref, up_ref, *rest):
    outs, sems = rest[:group_count], rest[group_count]
    local_total, _, cols = down_ref.shape
    blocks = ids_ref.shape[1]
    low = me_ref[0] * local_total
    copies = []
    for j in range(group_count):
        slots, seen = [jnp.int32(0)] * CAP, jnp.int32(0)
        for b in range(blocks):
            local = ids_ref[j, b] - low
            mine = (local >= 0) & (local < local_total)
            slots = [jnp.where(mine & (seen == r), local, s) for r, s in enumerate(slots)]
            seen = seen + mine.astype(jnp.int32)
        for r, slot in enumerate(slots):
            copies += [
                pltpu.make_async_copy(down_ref.at[slot], outs[j].at[r, :, pl.ds(0, cols)], sems.at[0, j, r]),
                pltpu.make_async_copy(up_ref.at[slot], outs[j].at[r, :, pl.ds(cols, up_ref.shape[2])], sems.at[1, j, r]),
            ]
            copies[-2].start()
            copies[-1].start()
    for copy in copies:
        copy.wait()


def reduce_kernel(group_count, owner_ref, me_ref, tokens_ref, *rest):
    got, (reduced_ref, up_ref, held, sems) = rest[:group_count], rest[group_count:]
    blocks, rank, cols = held.shape[0], held.shape[1], tokens_ref.shape[1]
    for b in range(blocks):
        earlier = jnp.int32(0)
        for a in range(b):
            earlier = earlier + (owner_ref[a] == owner_ref[b]).astype(jnp.int32)
        away = owner_ref[b] ^ me_ref[0]
        for j in range(group_count):

            @pl.when(away == j)
            def _():
                pltpu.make_async_copy(got[j].at[earlier], held.at[b], sems.at[b]).start()

    for b in range(blocks):
        pltpu.make_async_copy(got[0].at[0], held.at[b], sems.at[b]).wait()
        reduced_ref[b] = lax.dot_general(
            held[b, :, :cols],
            tokens_ref[b * BLOCK : (b + 1) * BLOCK, :],
            (((1,), (1,)), ((), ())),
            preferred_element_type=jnp.float32,
        )
        up_ref[b] = held[b, :, cols:]


def adapter_part(tokens, down_tables, up_tables, block_owner, block_local):
    group_count, tp_count = lax.axis_size("grp"), lax.axis_size("tp")
    me = lax.axis_index("grp").astype(jnp.int32).reshape(1)
    owners = block_owner[:, 0]
    blocks = owners.shape[0]
    local_total, cols, rank = down_tables.shape
    out_cols = up_tables.shape[2]
    down_rows = jnp.transpose(down_tables, (0, 2, 1))
    ids = (owners * local_total + block_local).reshape(1, blocks)
    step = 1
    while step < group_count:
        there = lax.ppermute(ids, "grp", [(i, i ^ step) for i in range(group_count)])
        ids = jnp.concatenate([ids, there], axis=0)
        step *= 2
    wide = cols + out_cols
    packed = pl.pallas_call(
        functools.partial(pack_kernel, group_count),
        out_shape=[jax.ShapeDtypeStruct((CAP, rank, wide), jnp.bfloat16)] * group_count,
        grid_spec=pltpu.PrefetchScalarGridSpec(
            num_scalar_prefetch=2,
            in_specs=[HBM, HBM],
            out_specs=[HBM] * group_count,
            scratch_shapes=[pltpu.SemaphoreType.DMA((2, group_count, CAP))],
        ),
    )(ids, me, down_rows, up_tables)
    got = [packed[0]] + [
        lax.ppermute(packed[j], "grp", [(i, i ^ j) for i in range(group_count)]) for j in range(1, group_count)
    ]
    reduced, up_block = pl.pallas_call(
        functools.partial(reduce_kernel, group_count),
        out_shape=[
            jax.ShapeDtypeStruct((blocks, rank, BLOCK), jnp.float32),
            jax.ShapeDtypeStruct((blocks, rank, out_cols), jnp.bfloat16),
        ],
        grid_spec=pltpu.PrefetchScalarGridSpec(
            num_scalar_prefetch=2,
            in_specs=[pl.BlockSpec(memory_space=pltpu.VMEM)] + [HBM] * group_count,
            out_specs=[pl.BlockSpec(memory_space=pltpu.VMEM)] * 2,
            scratch_shapes=[
                pltpu.VMEM((blocks, rank, wide), jnp.bfloat16),
                pltpu.SemaphoreType.DMA((blocks,)),
            ],
        ),
    )(owners, me, tokens, *got)
    total = reduced
    for j in range(1, tp_count):
        total = total + lax.ppermute(reduced, "tp", [(i, i ^ j) for i in range(tp_count)])
    lowrank = jnp.einsum(
        "nrb,nro->nbo", total, up_block.astype(jnp.float32), precision=lax.Precision.HIGHEST
    )
    return lowrank.reshape(blocks * BLOCK, out_cols)


def base_part(tokens, base_weight):
    tp_count = lax.axis_size("tp")
    if tp_count != 4:
        partial_value = jnp.dot(tokens, base_weight, preferred_element_type=jnp.float32)
        return lax.psum_scatter(partial_value, "tp", scatter_dimension=1, tiled=True)
    z = lax.axis_index("tp")
    width = base_weight.shape[1] // tp_count

    def product(block):
        columns = lax.dynamic_slice_in_dim(base_weight, block * width, width, 1)
        return jnp.dot(tokens, columns, preferred_element_type=jnp.float32)

    def code(value):
        return (value * SEND_SCALE).astype(jnp.float16)

    def plain(value):
        return value.astype(jnp.float32) * (1.0 / SEND_SCALE)

    far = code(product(z ^ 3))
    to_inner = lax.ppermute(far, "tp", [(0, 1), (3, 2)])
    from_inner = lax.ppermute(far, "tp", [(1, 2), (2, 1)])
    near = lax.ppermute(code(product(z ^ 1)), "tp", [(0, 1), (1, 0), (2, 3), (3, 2)])
    middle = code(product(z ^ 2) + plain(to_inner))
    middle = lax.ppermute(middle, "tp", [(0, 2), (2, 0), (1, 3), (3, 1)])
    return product(z) + (plain(from_inner) + plain(near) + plain(middle))


def body(tokens, base_weight, down_tables, up_tables, block_owner, block_local, block_count):
    base_projection = base_part(tokens, base_weight)
    lowrank = adapter_part(tokens, down_tables, up_tables, block_owner, block_local)
    offsets = jnp.arange(BLOCK, dtype=jnp.int32)
    live_rows = (offsets[None, :] < block_count[:, None]).reshape(tokens.shape[0], 1)
    combined_output = base_projection + adapter_scale * lowrank
    return jnp.where(live_rows, combined_output, jnp.float32(0.0)).astype(jnp.bfloat16)


def solution(mesh):
    placed = (
        P("grp", "tp"),
        P("tp", None),
        P("grp", "tp", None),
        P("grp", None, "tp"),
        P("grp", None),
        P("grp"),
        P("grp"),
    )
    return jax.shard_map(body, mesh=mesh, in_specs=placed, out_specs=P("grp", "tp"), check_vma=False)
```

```python
import functools

import jax
import jax.numpy as jnp
from jax import lax
from jax.experimental import pallas as pl
from jax.experimental.pallas import tpu as pltpu
from jax.experimental.layout import Layout, with_layout_constraint
from jax.sharding import PartitionSpec as P

BLOCK = 128
CAP = 2
adapter_scale = 2.0
SEND_SCALE = 16.0
HBM = pl.BlockSpec(memory_space=pl.ANY)


def pack_kernel(ids_ref, me_ref, down_ref, up_ref, out_ref, held, read_sems, write_sem):
    groups, blocks = ids_ref.shape
    local_total, _, cols = down_ref.shape
    low = me_ref[0] * local_total
    wanted = []
    for j in range(groups):
        slots, seen = [jnp.int32(0)] * CAP, jnp.int32(0)
        for b in range(blocks):
            local = ids_ref[j, b] - low
            mine = (local >= 0) & (local < local_total)
            slots = [jnp.where(mine & (seen == r), local, s) for r, s in enumerate(slots)]
            seen = seen + mine.astype(jnp.int32)
        for r, slot in enumerate(slots):
            k = j * CAP + r
            reads = [
                pltpu.make_async_copy(down_ref.at[slot], held.at[k, :, pl.ds(0, cols)], read_sems.at[k]),
                pltpu.make_async_copy(up_ref.at[slot], held.at[k, :, pl.ds(cols, up_ref.shape[2])], read_sems.at[k]),
            ]
            write = pltpu.make_async_copy(held.at[k], out_ref.at[me_ref[0] ^ j, r], write_sem)
            wanted.append((seen > r, reads, write))

            @pl.when(seen > r)
            def _():
                reads[0].start()
                reads[1].start()

    for there, reads, write in wanted:

        @pl.when(there)
        def _():
            reads[0].wait()
            reads[1].wait()
            write.start()

    for there, reads, write in wanted:

        @pl.when(there)
        def _():
            write.wait()


def later_kernel(value_ref, out_ref, sem):
    copy = pltpu.make_async_copy(value_ref, out_ref, sem)
    copy.start()
    copy.wait()


LONG = pl.CostEstimate(flops=100_000_000_000, bytes_accessed=1, transcendentals=0)
CHEAP = pl.CostEstimate(flops=1, bytes_accessed=1, transcendentals=0)


def adapter_ids(block_owner, block_local, local_total):
    group_count = lax.axis_size("grp")
    ids = (block_owner[:, 0] * local_total + block_local).reshape(1, block_owner.shape[0])
    step = 1
    while step < group_count:
        there = lax.ppermute(ids, "grp", [(i, i ^ step) for i in range(group_count)])
        ids = jnp.concatenate([ids, there], axis=0)
        yield ids
        step *= 2


def fetch_adapters(ids, down_tables, up_tables):
    group_count = lax.axis_size("grp")
    me = lax.axis_index("grp").astype(jnp.int32).reshape(1)
    _, cols, rank = down_tables.shape
    wide = cols + up_tables.shape[2]
    packed = pl.pallas_call(
        pack_kernel,
        out_shape=jax.ShapeDtypeStruct((group_count, CAP, rank, wide), jnp.bfloat16),
        grid_spec=pltpu.PrefetchScalarGridSpec(
            num_scalar_prefetch=2,
            in_specs=[HBM, HBM],
            out_specs=HBM,
            scratch_shapes=[
                pltpu.VMEM((group_count * CAP, rank, wide), jnp.bfloat16),
                pltpu.SemaphoreType.DMA((group_count * CAP,)),
                pltpu.SemaphoreType.DMA,
            ],
        ),
        cost_estimate=CHEAP,
    )(ids, me, jnp.transpose(down_tables, (0, 2, 1)), up_tables)
    got = lax.all_to_all(packed, "grp", split_axis=0, concat_axis=0, tiled=True)
    return got.reshape(group_count * CAP, rank, wide)


def later(value, *others):
    value = lax.optimization_barrier((value, *others))[0]
    return pl.pallas_call(
        later_kernel,
        out_shape=jax.ShapeDtypeStruct(value.shape, value.dtype),
        in_specs=[HBM],
        out_specs=HBM,
        scratch_shapes=[pltpu.SemaphoreType.DMA],
        cost_estimate=LONG,
    )(value)


def reduce_tokens(tokens, got, owners):
    blocks, cols = owners.shape[0], tokens.shape[1]
    order = jnp.arange(blocks, dtype=jnp.int32)
    earlier = (owners[None, :] == owners[:, None]) & (order[None, :] < order[:, None])
    block_slot = owners * CAP + jnp.sum(earlier.astype(jnp.int32), axis=1)
    mine = jnp.take(got, block_slot, axis=0, mode="clip")
    blocked = tokens.reshape(blocks, BLOCK, cols)
    reduced = jnp.einsum("nbd,nrd->nrb", blocked, mine[:, :, :cols], preferred_element_type=jnp.float32)
    return reduced, mine[:, :, cols:]


def body(tokens, base_weight, down_tables, up_tables, block_owner, block_local, block_count):
    tp_count = lax.axis_size("tp")
    z = lax.axis_index("tp")
    width = base_weight.shape[1] // tp_count
    owners = block_owner[:, 0]
    offsets = jnp.arange(BLOCK, dtype=jnp.int32)
    live_rows = (offsets[None, :] < block_count[:, None]).reshape(tokens.shape[0], 1)

    def product(block):
        columns = lax.dynamic_slice_in_dim(base_weight, block * width, width, 1)
        value = jnp.dot(tokens, columns, preferred_element_type=jnp.float32)
        return with_layout_constraint(value, Layout((0, 1)))

    def code(value):
        return (value * SEND_SCALE).astype(jnp.float16)

    def plain(value):
        return value.astype(jnp.float32) * (1.0 / SEND_SCALE)

    def after(value, *others):
        return lax.optimization_barrier((value, *others))[0]

    id_steps = list(adapter_ids(block_owner, block_local, down_tables.shape[0]))
    got = fetch_adapters(id_steps[-1], down_tables, up_tables)
    if tp_count == 4:
        far = code(product(z ^ 3))
        to_inner = lax.ppermute(far, "tp", [(0, 1), (3, 2)])
        from_inner = lax.ppermute(far, "tp", [(1, 2), (2, 1)])
        middle = product(after(z, id_steps[0]) ^ 2)
        middle, middle_code = lax.optimization_barrier((middle, code(middle)))
        from_middle = lax.ppermute(middle_code, "tp", [(0, 2), (3, 1)])
        near = code(product(after(z, id_steps[1]) ^ 1))
        from_near = lax.ppermute(near, "tp", [(0, 1), (1, 0), (2, 3), (3, 2)])
        inner_sum = code(middle + plain(to_inner))
        from_far = lax.ppermute(inner_sum, "tp", [(1, 3), (2, 0)])
        base_projection = lax.optimization_barrier(product(z) + plain(from_inner) + plain(from_middle))
        reduced, up_block = reduce_tokens(tokens, got, later(owners, base_projection))
        base_projection = lax.optimization_barrier(base_projection + (plain(from_near) + plain(from_far)))
    else:
        partial_value = jnp.dot(tokens, base_weight, preferred_element_type=jnp.float32)
        base_projection = lax.psum_scatter(partial_value, "tp", scatter_dimension=1, tiled=True)
        reduced, up_block = reduce_tokens(tokens, got, owners)
    total = reduced
    for j in range(1, tp_count):
        total = total + lax.ppermute(reduced, "tp", [(i, i ^ j) for i in range(tp_count)])
    lowrank = jnp.einsum(
        "nrb,nro->nbo", total, up_block.astype(jnp.float32), precision=lax.Precision.HIGHEST
    )
    combined_output = base_projection + adapter_scale * lowrank.reshape(base_projection.shape)
    return jnp.where(live_rows, combined_output, jnp.float32(0.0)).astype(jnp.bfloat16)


def solution(mesh):
    placed = (
        P("grp", "tp"),
        P("tp", None),
        P("grp", "tp", None),
        P("grp", None, "tp"),
        P("grp", None),
        P("grp"),
        P("grp"),
    )
    return jax.shard_map(body, mesh=mesh, in_specs=placed, out_specs=P("grp", "tp"), check_vma=False)
```

```python
import functools

import jax
import jax.numpy as jnp
from jax import lax
from jax.experimental import pallas as pl
from jax.experimental.pallas import tpu as pltpu
from jax.experimental.layout import Layout, with_layout_constraint
from jax.sharding import PartitionSpec as P

BLOCK = 128
CAP = 2
adapter_scale = 2.0
SEND_SCALE = 16.0
HBM = pl.BlockSpec(memory_space=pl.ANY)


def pack_kernel(ids_ref, me_ref, down_ref, up_ref, out_ref, held, read_sems, write_sem):
    groups, blocks = ids_ref.shape
    local_total, _, cols = down_ref.shape
    low = me_ref[0] * local_total
    wanted = []
    for j in range(groups):
        slots, seen = [jnp.int32(0)] * CAP, jnp.int32(0)
        for b in range(blocks):
            local = ids_ref[j, b] - low
            mine = (local >= 0) & (local < local_total)
            slots = [jnp.where(mine & (seen == r), local, s) for r, s in enumerate(slots)]
            seen = seen + mine.astype(jnp.int32)
        for r, slot in enumerate(slots):
            k = j * CAP + r
            reads = [
                pltpu.make_async_copy(down_ref.at[slot], held.at[k, :, pl.ds(0, cols)], read_sems.at[k]),
                pltpu.make_async_copy(up_ref.at[slot], held.at[k, :, pl.ds(cols, up_ref.shape[2])], read_sems.at[k]),
            ]
            write = pltpu.make_async_copy(held.at[k], out_ref.at[me_ref[0] ^ j, r], write_sem)
            wanted.append((seen > r, reads, write))

            @pl.when(seen > r)
            def _():
                reads[0].start()
                reads[1].start()

    for there, reads, write in wanted:

        @pl.when(there)
        def _():
            reads[0].wait()
            reads[1].wait()
            write.start()

    for there, reads, write in wanted:

        @pl.when(there)
        def _():
            write.wait()


def later_kernel(value_ref, out_ref, sem):
    copy = pltpu.make_async_copy(value_ref, out_ref, sem)
    copy.start()
    copy.wait()


LONG = pl.CostEstimate(flops=100_000_000_000, bytes_accessed=1, transcendentals=0)
CHEAP = pl.CostEstimate(flops=1, bytes_accessed=1, transcendentals=0)


def adapter_ids(block_owner, block_local, local_total):
    group_count = lax.axis_size("grp")
    ids = (block_owner[:, 0] * local_total + block_local).reshape(1, block_owner.shape[0])
    step = 1
    while step < group_count:
        there = lax.ppermute(ids, "grp", [(i, i ^ step) for i in range(group_count)])
        ids = jnp.concatenate([ids, there], axis=0)
        yield ids
        step *= 2


def pack_adapters(ids, down_tables, up_tables):
    group_count = lax.axis_size("grp")
    me = lax.axis_index("grp").astype(jnp.int32).reshape(1)
    _, cols, rank = down_tables.shape
    wide = cols + up_tables.shape[2]
    return pl.pallas_call(
        pack_kernel,
        out_shape=jax.ShapeDtypeStruct((group_count, CAP, rank, wide), jnp.bfloat16),
        grid_spec=pltpu.PrefetchScalarGridSpec(
            num_scalar_prefetch=2,
            in_specs=[HBM, HBM],
            out_specs=HBM,
            scratch_shapes=[
                pltpu.VMEM((group_count * CAP, rank, wide), jnp.bfloat16),
                pltpu.SemaphoreType.DMA((group_count * CAP,)),
                pltpu.SemaphoreType.DMA,
            ],
        ),
        cost_estimate=CHEAP,
    )(ids, me, jnp.transpose(down_tables, (0, 2, 1)), up_tables)


def exchange(packed):
    got = lax.all_to_all(packed, "grp", split_axis=0, concat_axis=0, tiled=True)
    return got.reshape(got.shape[0] * CAP, *got.shape[2:])


def later(value, *others):
    value = lax.optimization_barrier((value, *others))[0]
    return pl.pallas_call(
        later_kernel,
        out_shape=jax.ShapeDtypeStruct(value.shape, value.dtype),
        in_specs=[HBM],
        out_specs=HBM,
        scratch_shapes=[pltpu.SemaphoreType.DMA],
        cost_estimate=LONG,
    )(value)


def slot_plan(owners):
    order = jnp.arange(owners.shape[0], dtype=jnp.int32)
    earlier = (owners[None, :] == owners[:, None]) & (order[None, :] < order[:, None])
    return owners * CAP + jnp.sum(earlier.astype(jnp.int32), axis=1)


def reduce_tokens(tokens, got, block_slot):
    blocks, cols = block_slot.shape[0], tokens.shape[1]
    mine = jnp.take(got, block_slot, axis=0, mode="clip")
    mine = lax.optimization_barrier(mine)
    down_block = lax.optimization_barrier(mine[:, :, :cols])
    blocked = tokens.reshape(blocks, BLOCK, cols)
    reduced = jnp.einsum("nbd,nrd->nrb", blocked, down_block, preferred_element_type=jnp.float32)
    up_block, _ = lax.optimization_barrier((mine[:, :, cols:], reduced))
    return reduced, up_block


def body(tokens, base_weight, down_tables, up_tables, block_owner, block_local, block_count):
    tp_count = lax.axis_size("tp")
    z = lax.axis_index("tp")
    width = base_weight.shape[1] // tp_count
    owners = block_owner[:, 0]
    offsets = jnp.arange(BLOCK, dtype=jnp.int32)
    live_rows = (offsets[None, :] < block_count[:, None]).reshape(tokens.shape[0], 1)

    def product(block):
        columns = lax.dynamic_slice_in_dim(base_weight, block * width, width, 1)
        value = jnp.dot(tokens, columns, preferred_element_type=jnp.float32)
        return with_layout_constraint(value, Layout((0, 1)))

    def code(value):
        return (value * SEND_SCALE).astype(jnp.float16)

    def plain(value):
        return value.astype(jnp.float32) * (1.0 / SEND_SCALE)

    def after(value, *others):
        return lax.optimization_barrier((value, *others))[0]

    id_steps = list(adapter_ids(block_owner, block_local, down_tables.shape[0]))
    if tp_count == 4:
        end = (z == 0) | (z == 3)
        far = after(code(product(z ^ 3)), id_steps[0])
        to_inner = lax.ppermute(far, "tp", [(0, 1), (3, 2)])
        from_inner = lax.ppermute(far, "tp", [(1, 2), (2, 1)])
        later_z = after(z, id_steps[1])
        first = code(product(later_z ^ jnp.where(end, 2, 1)))
        from_first = lax.ppermute(first, "tp", [(0, 2), (3, 1), (1, 0), (2, 3)])
        packed = pack_adapters(after(id_steps[-1], first), down_tables, up_tables)
        later_z, packed = lax.optimization_barrier((z, packed))
        got = exchange(packed)
        second = product(later_z ^ jnp.where(end, 1, 2))
        second = code(second + plain(to_inner))
        from_second = lax.ppermute(second, "tp", [(0, 1), (3, 2), (1, 3), (2, 0)])
        own = lax.optimization_barrier(product(after(z, second)))
        base_projection = lax.optimization_barrier(own + plain(from_inner) + plain(from_first))
        block_slot = slot_plan(later(owners, base_projection))
        reduced, up_block = reduce_tokens(tokens, got, block_slot)
        from_second = after(from_second, reduced)
        base_projection = lax.optimization_barrier(base_projection + plain(from_second))
    else:
        partial_value = jnp.dot(tokens, base_weight, preferred_element_type=jnp.float32)
        base_projection = lax.psum_scatter(partial_value, "tp", scatter_dimension=1, tiled=True)
        got = exchange(pack_adapters(id_steps[-1], down_tables, up_tables))
        reduced, up_block = reduce_tokens(tokens, got, slot_plan(owners))
    total = reduced
    for j in range(1, tp_count):
        total = total + lax.ppermute(reduced, "tp", [(i, i ^ j) for i in range(tp_count)])
    lowrank = jnp.einsum(
        "nrb,nro->nbo", total, up_block.astype(jnp.float32), precision=lax.Precision.HIGHEST
    )
    combined_output = base_projection + adapter_scale * lowrank.reshape(base_projection.shape)
    return jnp.where(live_rows, combined_output, jnp.float32(0.0)).astype(jnp.bfloat16)


def solution(mesh):
    placed = (
        P("grp", "tp"),
        P("tp", None),
        P("grp", "tp", None),
        P("grp", None, "tp"),
        P("grp", None),
        P("grp"),
        P("grp"),
    )
    return jax.shard_map(body, mesh=mesh, in_specs=placed, out_specs=P("grp", "tp"), check_vma=False)
```

```python
import functools

import jax
import jax.numpy as jnp
from jax import lax
from jax.experimental import pallas as pl
from jax.experimental.pallas import tpu as pltpu
from jax.experimental.layout import Layout, with_layout_constraint
from jax.sharding import PartitionSpec as P

BLOCK = 128
CAP = 2
adapter_scale = 2.0
SEND_SCALE = 16.0
HBM = pl.BlockSpec(memory_space=pl.ANY)


def pack_kernel(ids_ref, me_ref, down_ref, up_ref, out_ref, held, read_sems, write_sem):
    groups, blocks = ids_ref.shape
    local_total, _, cols = down_ref.shape
    low = me_ref[0] * local_total
    wanted = []
    for j in range(groups):
        slots, seen = [jnp.int32(0)] * CAP, jnp.int32(0)
        for b in range(blocks):
            local = ids_ref[j, b] - low
            mine = (local >= 0) & (local < local_total)
            slots = [jnp.where(mine & (seen == r), local, s) for r, s in enumerate(slots)]
            seen = seen + mine.astype(jnp.int32)
        for r, slot in enumerate(slots):
            k = j * CAP + r
            reads = [
                pltpu.make_async_copy(down_ref.at[slot], held.at[k, :, pl.ds(0, cols)], read_sems.at[k]),
                pltpu.make_async_copy(up_ref.at[slot], held.at[k, :, pl.ds(cols, up_ref.shape[2])], read_sems.at[k]),
            ]
            write = pltpu.make_async_copy(held.at[k], out_ref.at[me_ref[0] ^ j, r], write_sem)
            wanted.append((seen > r, reads, write))

            @pl.when(seen > r)
            def _():
                reads[0].start()
                reads[1].start()

    for there, reads, write in wanted:

        @pl.when(there)
        def _():
            reads[0].wait()
            reads[1].wait()
            write.start()

    for there, reads, write in wanted:

        @pl.when(there)
        def _():
            write.wait()


def later_kernel(value_ref, out_ref, sem):
    copy = pltpu.make_async_copy(value_ref, out_ref, sem)
    copy.start()
    copy.wait()


LONG = pl.CostEstimate(flops=100_000_000_000, bytes_accessed=1, transcendentals=0)
CHEAP = pl.CostEstimate(flops=1, bytes_accessed=1, transcendentals=0)


def adapter_ids(block_owner, block_local, local_total):
    group_count = lax.axis_size("grp")
    ids = (block_owner[:, 0] * local_total + block_local).reshape(1, block_owner.shape[0])
    step = 1
    while step < group_count:
        there = lax.ppermute(ids, "grp", [(i, i ^ step) for i in range(group_count)])
        ids = jnp.concatenate([ids, there], axis=0)
        yield ids
        step *= 2


def pack_adapters(ids, down_tables, up_tables):
    group_count = lax.axis_size("grp")
    me = lax.axis_index("grp").astype(jnp.int32).reshape(1)
    _, cols, rank = down_tables.shape
    wide = cols + up_tables.shape[2]
    return pl.pallas_call(
        pack_kernel,
        out_shape=jax.ShapeDtypeStruct((group_count, CAP, rank, wide), jnp.bfloat16),
        grid_spec=pltpu.PrefetchScalarGridSpec(
            num_scalar_prefetch=2,
            in_specs=[HBM, HBM],
            out_specs=HBM,
            scratch_shapes=[
                pltpu.VMEM((group_count * CAP, rank, wide), jnp.bfloat16),
                pltpu.SemaphoreType.DMA((group_count * CAP,)),
                pltpu.SemaphoreType.DMA,
            ],
        ),
        cost_estimate=CHEAP,
    )(ids, me, jnp.transpose(down_tables, (0, 2, 1)), up_tables)


def exchange(packed):
    got = lax.all_to_all(packed, "grp", split_axis=0, concat_axis=0, tiled=True)
    return got.reshape(got.shape[0] * CAP, *got.shape[2:])


def later(value, *others):
    value = lax.optimization_barrier((value, *others))[0]
    return pl.pallas_call(
        later_kernel,
        out_shape=jax.ShapeDtypeStruct(value.shape, value.dtype),
        in_specs=[HBM],
        out_specs=HBM,
        scratch_shapes=[pltpu.SemaphoreType.DMA],
        cost_estimate=LONG,
    )(value)


def slot_plan(owners):
    order = jnp.arange(owners.shape[0], dtype=jnp.int32)
    earlier = (owners[None, :] == owners[:, None]) & (order[None, :] < order[:, None])
    return owners * CAP + jnp.sum(earlier.astype(jnp.int32), axis=1)


def reduce_tokens(tokens, got, block_slot):
    blocks, cols = block_slot.shape[0], tokens.shape[1]
    mine = jnp.take(got, block_slot, axis=0, mode="clip")
    mine = lax.optimization_barrier(mine)
    down_block = lax.optimization_barrier(mine[:, :, :cols])
    blocked = tokens.reshape(blocks, BLOCK, cols)
    reduced = jnp.einsum("nbd,nrd->nrb", blocked, down_block, preferred_element_type=jnp.float32)
    up_block, _ = lax.optimization_barrier((mine[:, :, cols:], reduced))
    return reduced, up_block


def body(tokens, base_weight, down_tables, up_tables, block_owner, block_local, block_count):
    tp_count = lax.axis_size("tp")
    z = lax.axis_index("tp")
    width = base_weight.shape[1] // tp_count
    owners = block_owner[:, 0]

    def product(block):
        columns = lax.dynamic_slice_in_dim(base_weight, block * width, width, 1)
        value = jnp.dot(tokens, columns, preferred_element_type=jnp.float32)
        return with_layout_constraint(value, Layout((0, 1)))

    def code(value):
        return (value * SEND_SCALE).astype(jnp.float16)

    def plain(value):
        return value.astype(jnp.float32) * (1.0 / SEND_SCALE)

    def after(value, *others):
        return lax.optimization_barrier((value, *others))[0]

    id_steps = list(adapter_ids(block_owner, block_local, down_tables.shape[0]))
    live_counts = block_count
    if tp_count == 4:
        end = (z == 0) | (z == 3)
        far = after(code(product(z ^ 3)), id_steps[0])
        to_inner = lax.ppermute(far, "tp", [(0, 1), (3, 2)])
        from_inner = lax.ppermute(far, "tp", [(1, 2), (2, 1)])
        later_z = after(z, id_steps[1])
        first = code(product(later_z ^ jnp.where(end, 2, 1)))
        from_first = lax.ppermute(first, "tp", [(0, 2), (3, 1), (1, 0), (2, 3)])
        packed = pack_adapters(after(id_steps[-1], first), down_tables, up_tables)
        later_z, packed = lax.optimization_barrier((z, packed))
        got = exchange(packed)
        second = product(later_z ^ jnp.where(end, 1, 2))
        second = code(second + plain(to_inner))
        from_second = lax.ppermute(second, "tp", [(0, 1), (3, 2), (1, 3), (2, 0)])
        own = lax.optimization_barrier(product(after(z, second)))
        live_counts = after(block_count, own)
        base_projection = lax.optimization_barrier(own + plain(from_inner) + plain(from_first))
        block_slot = slot_plan(later(owners, base_projection))
        reduced, up_block = reduce_tokens(tokens, got, block_slot)
        from_second = after(from_second, reduced)
        base_projection = lax.optimization_barrier(base_projection + plain(from_second))
    else:
        partial_value = jnp.dot(tokens, base_weight, preferred_element_type=jnp.float32)
        base_projection = lax.psum_scatter(partial_value, "tp", scatter_dimension=1, tiled=True)
        got = exchange(pack_adapters(id_steps[-1], down_tables, up_tables))
        reduced, up_block = reduce_tokens(tokens, got, slot_plan(owners))
    total = reduced
    for j in range(1, tp_count):
        total = total + lax.ppermute(reduced, "tp", [(i, i ^ j) for i in range(tp_count)])
    lowrank = jnp.einsum(
        "nrb,nro->nbo", total, up_block.astype(jnp.float32), precision=lax.Precision.HIGHEST
    )
    offsets = jnp.arange(BLOCK, dtype=jnp.int32)
    live_rows = offsets[None, :, None] < live_counts[:, None, None]
    combined_output = base_projection.reshape(lowrank.shape) + adapter_scale * lowrank
    projected = jnp.where(live_rows, combined_output, jnp.float32(0.0)).astype(jnp.bfloat16)
    return projected.reshape(base_projection.shape)


def solution(mesh):
    placed = (
        P("grp", "tp"),
        P("tp", None),
        P("grp", "tp", None),
        P("grp", None, "tp"),
        P("grp", None),
        P("grp"),
        P("grp"),
    )
    return jax.shard_map(body, mesh=mesh, in_specs=placed, out_specs=P("grp", "tp"), check_vma=False)
```

```python
import functools

import jax
import jax.numpy as jnp
from jax import lax
from jax.experimental import pallas as pl
from jax.experimental.pallas import tpu as pltpu
from jax.experimental.layout import Layout, with_layout_constraint
from jax.sharding import PartitionSpec as P

BLOCK = 128
CAP = 2
adapter_scale = 2.0
SEND_SCALE = 16.0
HBM = pl.BlockSpec(memory_space=pl.ANY)


def pack_kernel(ids_ref, me_ref, down_ref, up_ref, out_ref, held, read_sems, write_sem):
    groups, blocks = ids_ref.shape
    local_total, _, cols = down_ref.shape
    low = me_ref[0] * local_total
    wanted = []
    for j in range(groups):
        slots, seen = [jnp.int32(0)] * CAP, jnp.int32(0)
        for b in range(blocks):
            local = ids_ref[j, b] - low
            mine = (local >= 0) & (local < local_total)
            slots = [jnp.where(mine & (seen == r), local, s) for r, s in enumerate(slots)]
            seen = seen + mine.astype(jnp.int32)
        for r, slot in enumerate(slots):
            k = j * CAP + r
            reads = [
                pltpu.make_async_copy(down_ref.at[slot], held.at[k, :, pl.ds(0, cols)], read_sems.at[k]),
                pltpu.make_async_copy(up_ref.at[slot], held.at[k, :, pl.ds(cols, up_ref.shape[2])], read_sems.at[k]),
            ]
            write = pltpu.make_async_copy(held.at[k], out_ref.at[me_ref[0] ^ j, r], write_sem)
            wanted.append((seen > r, reads, write))

            @pl.when(seen > r)
            def _():
                reads[0].start()
                reads[1].start()

    for there, reads, write in wanted:

        @pl.when(there)
        def _():
            reads[0].wait()
            reads[1].wait()
            write.start()

    for there, reads, write in wanted:

        @pl.when(there)
        def _():
            write.wait()


def later_kernel(value_ref, out_ref, sem):
    copy = pltpu.make_async_copy(value_ref, out_ref, sem)
    copy.start()
    copy.wait()


LONG = pl.CostEstimate(flops=100_000_000_000, bytes_accessed=1, transcendentals=0)
CHEAP = pl.CostEstimate(flops=1, bytes_accessed=1, transcendentals=0)


def adapter_ids(block_owner, block_local, local_total):
    group_count = lax.axis_size("grp")
    ids = (block_owner[:, 0] * local_total + block_local).reshape(1, block_owner.shape[0])
    step = 1
    while step < group_count:
        there = lax.ppermute(ids, "grp", [(i, i ^ step) for i in range(group_count)])
        ids = jnp.concatenate([ids, there], axis=0)
        yield ids
        step *= 2


def pack_adapters(ids, down_tables, up_tables):
    group_count = lax.axis_size("grp")
    me = lax.axis_index("grp").astype(jnp.int32).reshape(1)
    _, cols, rank = down_tables.shape
    wide = cols + up_tables.shape[2]
    return pl.pallas_call(
        pack_kernel,
        out_shape=jax.ShapeDtypeStruct((group_count, CAP, rank, wide), jnp.bfloat16),
        grid_spec=pltpu.PrefetchScalarGridSpec(
            num_scalar_prefetch=2,
            in_specs=[HBM, HBM],
            out_specs=HBM,
            scratch_shapes=[
                pltpu.VMEM((group_count * CAP, rank, wide), jnp.bfloat16),
                pltpu.SemaphoreType.DMA((group_count * CAP,)),
                pltpu.SemaphoreType.DMA,
            ],
        ),
        cost_estimate=CHEAP,
    )(ids, me, jnp.transpose(down_tables, (0, 2, 1)), up_tables)


def exchange(packed):
    got = lax.all_to_all(packed, "grp", split_axis=0, concat_axis=0, tiled=True)
    return got.reshape(got.shape[0] * CAP, *got.shape[2:])


def later(value, *others):
    value = lax.optimization_barrier((value, *others))[0]
    return pl.pallas_call(
        later_kernel,
        out_shape=jax.ShapeDtypeStruct(value.shape, value.dtype),
        in_specs=[HBM],
        out_specs=HBM,
        scratch_shapes=[pltpu.SemaphoreType.DMA],
        cost_estimate=LONG,
    )(value)


def slot_plan(owners):
    order = jnp.arange(owners.shape[0], dtype=jnp.int32)
    earlier = (owners[None, :] == owners[:, None]) & (order[None, :] < order[:, None])
    return owners * CAP + jnp.sum(earlier.astype(jnp.int32), axis=1)


def reduce_tokens(tokens, got, block_slot):
    blocks, cols = block_slot.shape[0], tokens.shape[1]
    mine = jnp.take(got, block_slot, axis=0, mode="clip")
    mine = lax.optimization_barrier(mine)
    down_block = lax.optimization_barrier(mine[:, :, :cols])
    blocked = tokens.reshape(blocks, BLOCK, cols)
    reduced = jnp.einsum("nbd,nrd->nrb", blocked, down_block, preferred_element_type=jnp.float32)
    up_block, _ = lax.optimization_barrier((mine[:, :, cols:], reduced))
    return reduced, up_block


def body(tokens, base_weight, down_tables, up_tables, block_owner, block_local, block_count):
    tp_count = lax.axis_size("tp")
    z = lax.axis_index("tp")
    width = base_weight.shape[1] // tp_count
    owners = block_owner[:, 0]

    def product(block):
        columns = lax.dynamic_slice_in_dim(base_weight, block * width, width, 1)
        value = jnp.dot(tokens, columns, preferred_element_type=jnp.float32)
        return with_layout_constraint(value, Layout((0, 1)))

    def code(value):
        return (value * SEND_SCALE).astype(jnp.float16)

    def plain(value):
        return value.astype(jnp.float32) * (1.0 / SEND_SCALE)

    def after(value, *others):
        return lax.optimization_barrier((value, *others))[0]

    id_steps = list(adapter_ids(block_owner, block_local, down_tables.shape[0]))
    live_counts = block_count
    if tp_count == 4:
        end = (z == 0) | (z == 3)
        far = after(code(product(z ^ 3)), id_steps[0])
        to_inner = lax.ppermute(far, "tp", [(0, 1), (3, 2)])
        from_inner = lax.ppermute(far, "tp", [(1, 2), (2, 1)])
        later_z = after(z, id_steps[1])
        first = code(product(later_z ^ jnp.where(end, 2, 1)))
        from_first = lax.ppermute(first, "tp", [(0, 2), (3, 1), (1, 0), (2, 3)])
        packed = pack_adapters(after(id_steps[-1], first), down_tables, up_tables)
        later_z, packed = lax.optimization_barrier((z, packed))
        got = exchange(packed)
        second = product(later_z ^ jnp.where(end, 1, 2))
        second = code(second + plain(to_inner))
        from_second = lax.ppermute(second, "tp", [(0, 1), (3, 2), (1, 3), (2, 0)])
        own = lax.optimization_barrier(product(after(z, second)))
        live_counts = after(block_count, own)
        base_projection = lax.optimization_barrier(own + plain(from_first))
        block_slot = slot_plan(later(owners, base_projection))
        reduced, up_block = reduce_tokens(tokens, got, block_slot)
        from_second = after(from_second, reduced)
        base_projection = lax.optimization_barrier(base_projection + plain(from_inner) + plain(from_second))
    else:
        partial_value = jnp.dot(tokens, base_weight, preferred_element_type=jnp.float32)
        base_projection = lax.psum_scatter(partial_value, "tp", scatter_dimension=1, tiled=True)
        got = exchange(pack_adapters(id_steps[-1], down_tables, up_tables))
        reduced, up_block = reduce_tokens(tokens, got, slot_plan(owners))
    total = reduced
    for j in range(1, tp_count):
        total = total + lax.ppermute(reduced, "tp", [(i, i ^ j) for i in range(tp_count)])
    lowrank = jnp.einsum(
        "nrb,nro->nbo", total, up_block.astype(jnp.float32), precision=lax.Precision.HIGHEST
    )
    offsets = jnp.arange(BLOCK, dtype=jnp.int32)
    live_rows = offsets[None, :, None] < live_counts[:, None, None]
    combined_output = base_projection.reshape(lowrank.shape) + adapter_scale * lowrank
    projected = jnp.where(live_rows, combined_output, jnp.float32(0.0)).astype(jnp.bfloat16)
    return projected.reshape(base_projection.shape)


def solution(mesh):
    placed = (
        P("grp", "tp"),
        P("tp", None),
        P("grp", "tp", None),
        P("grp", None, "tp"),
        P("grp", None),
        P("grp"),
        P("grp"),
    )
    return jax.shard_map(body, mesh=mesh, in_specs=placed, out_specs=P("grp", "tp"), check_vma=False)
```

```python
import math

import jax
import jax.numpy as jnp
from jax import lax
from jax.experimental import pallas as pl
from jax.experimental.pallas import tpu as pltpu
from jax.experimental.layout import Layout, with_layout_constraint
from jax.sharding import PartitionSpec as P

BLOCK = 128
CAP = 2
adapter_scale = 2.0
FLOAT16_MAX = 65504.0
PRODUCT_MAX = 6.0 * 0.0625
HBM = pl.BlockSpec(memory_space=pl.ANY)


def pack_kernel(ids_ref, me_ref, down_ref, up_ref, out_ref, held, read_sems, write_sem):
    groups, blocks = ids_ref.shape
    local_total, _, cols = down_ref.shape
    low = me_ref[0] * local_total
    wanted = []
    for j in range(groups):
        slots, seen = [jnp.int32(0)] * CAP, jnp.int32(0)
        for b in range(blocks):
            local = ids_ref[j, b] - low
            mine = (local >= 0) & (local < local_total)
            slots = [jnp.where(mine & (seen == r), local, s) for r, s in enumerate(slots)]
            seen = seen + mine.astype(jnp.int32)
        for r, slot in enumerate(slots):
            k = j * CAP + r
            reads = [
                pltpu.make_async_copy(down_ref.at[slot], held.at[k, :, pl.ds(0, cols)], read_sems.at[k]),
                pltpu.make_async_copy(up_ref.at[slot], held.at[k, :, pl.ds(cols, up_ref.shape[2])], read_sems.at[k]),
            ]
            write = pltpu.make_async_copy(held.at[k], out_ref.at[me_ref[0] ^ j, r], write_sem)
            wanted.append((seen > r, reads, write))

            @pl.when(seen > r)
            def _():
                reads[0].start()
                reads[1].start()

    for there, reads, write in wanted:

        @pl.when(there)
        def _():
            reads[0].wait()
            reads[1].wait()
            write.start()

    for there, reads, write in wanted:

        @pl.when(there)
        def _():
            write.wait()


def later_kernel(value_ref, out_ref, sem):
    copy = pltpu.make_async_copy(value_ref, out_ref, sem)
    copy.start()
    copy.wait()


LONG = pl.CostEstimate(flops=100_000_000_000, bytes_accessed=1, transcendentals=0)
CHEAP = pl.CostEstimate(flops=1, bytes_accessed=1, transcendentals=0)


def adapter_ids(block_owner, block_local, local_total):
    group_count = lax.axis_size("grp")
    ids = (block_owner[:, 0] * local_total + block_local).reshape(1, block_owner.shape[0])
    step = 1
    while step < group_count:
        there = lax.ppermute(ids, "grp", [(i, i ^ step) for i in range(group_count)])
        ids = jnp.concatenate([ids, there], axis=0)
        yield ids
        step *= 2


def pack_adapters(ids, down_tables, up_tables):
    group_count = lax.axis_size("grp")
    me = lax.axis_index("grp").astype(jnp.int32).reshape(1)
    _, cols, rank = down_tables.shape
    wide = cols + up_tables.shape[2]
    return pl.pallas_call(
        pack_kernel,
        out_shape=jax.ShapeDtypeStruct((group_count, CAP, rank, wide), jnp.bfloat16),
        grid_spec=pltpu.PrefetchScalarGridSpec(
            num_scalar_prefetch=2,
            in_specs=[HBM, HBM],
            out_specs=HBM,
            scratch_shapes=[
                pltpu.VMEM((group_count * CAP, rank, wide), jnp.bfloat16),
                pltpu.SemaphoreType.DMA((group_count * CAP,)),
                pltpu.SemaphoreType.DMA,
            ],
        ),
        cost_estimate=CHEAP,
    )(ids, me, jnp.transpose(down_tables, (0, 2, 1)), up_tables)


def exchange(packed):
    got = lax.all_to_all(packed, "grp", split_axis=0, concat_axis=0, tiled=True)
    return got.reshape(got.shape[0] * CAP, *got.shape[2:])


def later(value, *others):
    value = lax.optimization_barrier((value, *others))[0]
    return pl.pallas_call(
        later_kernel,
        out_shape=jax.ShapeDtypeStruct(value.shape, value.dtype),
        in_specs=[HBM],
        out_specs=HBM,
        scratch_shapes=[pltpu.SemaphoreType.DMA],
        cost_estimate=LONG,
    )(value)


def slot_plan(owners):
    order = jnp.arange(owners.shape[0], dtype=jnp.int32)
    earlier = (owners[None, :] == owners[:, None]) & (order[None, :] < order[:, None])
    return owners * CAP + jnp.sum(earlier.astype(jnp.int32), axis=1)


def reduce_tokens(tokens, got, block_slot):
    blocks, cols = block_slot.shape[0], tokens.shape[1]
    mine = jnp.take(got, block_slot, axis=0, mode="clip")
    mine = lax.optimization_barrier(mine)
    down_block = lax.optimization_barrier(mine[:, :, :cols])
    blocked = tokens.reshape(blocks, BLOCK, cols)
    reduced = jnp.einsum("nbd,nrd->nrb", blocked, down_block, preferred_element_type=jnp.float32)
    up_block, _ = lax.optimization_barrier((mine[:, :, cols:], reduced))
    return reduced, up_block


def expand_tokens(total, up_block):
    parts, rest = [], total
    for _ in range(3):
        part = lax.reduce_precision(rest, exponent_bits=8, mantissa_bits=7)
        parts.append(part.astype(jnp.bfloat16))
        rest = rest - part
    parts = jnp.concatenate(parts, axis=1)
    up_parts = jnp.concatenate([up_block] * 3, axis=1)
    return jnp.einsum("nrb,nro->nbo", parts, up_parts, preferred_element_type=jnp.float32)


def body(tokens, base_weight, down_tables, up_tables, block_owner, block_local, block_count):
    tp_count = lax.axis_size("tp")
    z = lax.axis_index("tp")
    width = base_weight.shape[1] // tp_count
    owners = block_owner[:, 0]

    def product(block):
        columns = lax.dynamic_slice_in_dim(base_weight, block * width, width, 1)
        value = jnp.dot(tokens, columns, preferred_element_type=jnp.float32)
        return with_layout_constraint(value, Layout((0, 1)))

    scale = 2.0 ** math.floor(math.log2(FLOAT16_MAX / (2 * tokens.shape[1] * PRODUCT_MAX)))

    def code(value):
        return (value * scale).astype(jnp.float16)

    def plain(value):
        return value.astype(jnp.float32) * (1.0 / scale)

    def after(value, *others):
        return lax.optimization_barrier((value, *others))[0]

    id_steps = list(adapter_ids(block_owner, block_local, down_tables.shape[0]))
    live_counts = block_count
    if tp_count == 4:
        end = (z == 0) | (z == 3)
        far = after(code(product(z ^ 3)), id_steps[0])
        to_inner = lax.ppermute(far, "tp", [(0, 1), (3, 2)])
        from_inner = lax.ppermute(far, "tp", [(1, 2), (2, 1)])
        later_z = after(z, id_steps[1])
        first = code(product(later_z ^ jnp.where(end, 2, 1)))
        from_first = lax.ppermute(first, "tp", [(0, 2), (3, 1), (1, 0), (2, 3)])
        packed = pack_adapters(after(id_steps[-1], first), down_tables, up_tables)
        later_z, packed = lax.optimization_barrier((z, packed))
        got = exchange(packed)
        second = product(later_z ^ jnp.where(end, 1, 2))
        second = code(second + plain(to_inner))
        from_second = lax.ppermute(second, "tp", [(0, 1), (3, 2), (1, 3), (2, 0)])
        own = lax.optimization_barrier(product(after(z, second)))
        live_counts = after(block_count, own)
        base_projection = lax.optimization_barrier(own + plain(from_first))
        block_slot = slot_plan(later(owners, base_projection))
        reduced, up_block = reduce_tokens(tokens, got, block_slot)
        from_second = after(from_second, reduced)
        base_projection = lax.optimization_barrier(base_projection + plain(from_inner) + plain(from_second))
    else:
        partial_value = jnp.dot(tokens, base_weight, preferred_element_type=jnp.float32)
        base_projection = lax.psum_scatter(partial_value, "tp", scatter_dimension=1, tiled=True)
        got = exchange(pack_adapters(id_steps[-1], down_tables, up_tables))
        reduced, up_block = reduce_tokens(tokens, got, slot_plan(owners))
    total = reduced
    for j in range(1, tp_count):
        total = total + lax.ppermute(reduced, "tp", [(i, i ^ j) for i in range(tp_count)])
    lowrank = expand_tokens(total, up_block)
    offsets = jnp.arange(BLOCK, dtype=jnp.int32)
    live_rows = offsets[None, :, None] < live_counts[:, None, None]
    combined_output = base_projection.reshape(lowrank.shape) + adapter_scale * lowrank
    projected = jnp.where(live_rows, combined_output, jnp.float32(0.0)).astype(jnp.bfloat16)
    return projected.reshape(base_projection.shape)


def solution(mesh):
    placed = (
        P("grp", "tp"),
        P("tp", None),
        P("grp", "tp", None),
        P("grp", None, "tp"),
        P("grp", None),
        P("grp"),
        P("grp"),
    )
    return jax.shard_map(body, mesh=mesh, in_specs=placed, out_specs=P("grp", "tp"), check_vma=False)
```

```python
import math

import jax
import jax.numpy as jnp
from jax import lax
from jax.experimental import pallas as pl
from jax.experimental.pallas import tpu as pltpu
from jax.experimental.layout import Layout, with_layout_constraint
from jax.sharding import PartitionSpec as P

BLOCK = 128
CAP = 2
adapter_scale = 2.0
FLOAT16_MAX = 65504.0
PRODUCT_MAX = 6.0 * 0.0625
HBM = pl.BlockSpec(memory_space=pl.ANY)


def pack_kernel(ids_ref, me_ref, down_ref, up_ref, out_ref, held, read_sems, write_sem):
    groups, blocks = ids_ref.shape
    local_total, _, cols = down_ref.shape
    low = me_ref[0] * local_total
    wanted = []
    for j in range(groups):
        slots, seen = [jnp.int32(0)] * CAP, jnp.int32(0)
        for b in range(blocks):
            local = ids_ref[j, b] - low
            mine = (local >= 0) & (local < local_total)
            slots = [jnp.where(mine & (seen == r), local, s) for r, s in enumerate(slots)]
            seen = seen + mine.astype(jnp.int32)
        for r, slot in enumerate(slots):
            k = j * CAP + r
            reads = [
                pltpu.make_async_copy(down_ref.at[slot], held.at[k, :, pl.ds(0, cols)], read_sems.at[k]),
                pltpu.make_async_copy(up_ref.at[slot], held.at[k, :, pl.ds(cols, up_ref.shape[2])], read_sems.at[k]),
            ]
            write = pltpu.make_async_copy(held.at[k], out_ref.at[me_ref[0] ^ j, r], write_sem)
            wanted.append((seen > r, reads, write))

            @pl.when(seen > r)
            def _():
                reads[0].start()
                reads[1].start()

    for there, reads, write in wanted:

        @pl.when(there)
        def _():
            reads[0].wait()
            reads[1].wait()
            write.start()

    for there, reads, write in wanted:

        @pl.when(there)
        def _():
            write.wait()


def later_kernel(value_ref, out_ref, sem):
    copy = pltpu.make_async_copy(value_ref, out_ref, sem)
    copy.start()
    copy.wait()


LONG = pl.CostEstimate(flops=100_000_000_000, bytes_accessed=1, transcendentals=0)
CHEAP = pl.CostEstimate(flops=1, bytes_accessed=1, transcendentals=0)


def adapter_ids(block_owner, block_local, local_total):
    group_count = lax.axis_size("grp")
    ids = (block_owner[:, 0] * local_total + block_local).reshape(1, block_owner.shape[0])
    step = 1
    while step < group_count:
        there = lax.ppermute(ids, "grp", [(i, i ^ step) for i in range(group_count)])
        ids = jnp.concatenate([ids, there], axis=0)
        yield ids
        step *= 2


def pack_adapters(ids, down_tables, up_tables):
    group_count = lax.axis_size("grp")
    me = lax.axis_index("grp").astype(jnp.int32).reshape(1)
    _, cols, rank = down_tables.shape
    wide = cols + up_tables.shape[2]
    return pl.pallas_call(
        pack_kernel,
        out_shape=jax.ShapeDtypeStruct((group_count, CAP, rank, wide), jnp.bfloat16),
        grid_spec=pltpu.PrefetchScalarGridSpec(
            num_scalar_prefetch=2,
            in_specs=[HBM, HBM],
            out_specs=HBM,
            scratch_shapes=[
                pltpu.VMEM((group_count * CAP, rank, wide), jnp.bfloat16),
                pltpu.SemaphoreType.DMA((group_count * CAP,)),
                pltpu.SemaphoreType.DMA,
            ],
        ),
        cost_estimate=CHEAP,
    )(ids, me, jnp.transpose(down_tables, (0, 2, 1)), up_tables)


def exchange(packed):
    got = lax.all_to_all(packed, "grp", split_axis=0, concat_axis=0, tiled=True)
    return got.reshape(got.shape[0] * CAP, *got.shape[2:])


def later(value, *others):
    value = lax.optimization_barrier((value, *others))[0]
    return pl.pallas_call(
        later_kernel,
        out_shape=jax.ShapeDtypeStruct(value.shape, value.dtype),
        in_specs=[HBM],
        out_specs=HBM,
        scratch_shapes=[pltpu.SemaphoreType.DMA],
        cost_estimate=LONG,
    )(value)


def slot_plan(owners):
    order = jnp.arange(owners.shape[0], dtype=jnp.int32)
    earlier = (owners[None, :] == owners[:, None]) & (order[None, :] < order[:, None])
    return owners * CAP + jnp.sum(earlier.astype(jnp.int32), axis=1)


def reduce_tokens(tokens, got, block_slot):
    blocks, cols = block_slot.shape[0], tokens.shape[1]
    match = block_slot[:, None] == jnp.arange(got.shape[0], dtype=jnp.int32)[None, :]
    mine = jnp.sum(jnp.where(match[:, :, None, None], got[None], jnp.bfloat16(0.0)).astype(jnp.float32), axis=1).astype(jnp.bfloat16)
    mine = lax.optimization_barrier(mine)
    down_block = lax.optimization_barrier(mine[:, :, :cols])
    blocked = tokens.reshape(blocks, BLOCK, cols)
    reduced = jnp.einsum("nbd,nrd->nrb", blocked, down_block, preferred_element_type=jnp.float32)
    up_block, _ = lax.optimization_barrier((mine[:, :, cols:], reduced))
    return reduced, up_block


def expand_tokens(total, up_block):
    parts, rest = [], total
    for _ in range(3):
        part = lax.reduce_precision(rest, exponent_bits=8, mantissa_bits=7)
        parts.append(part.astype(jnp.bfloat16))
        rest = rest - part
    parts = jnp.concatenate(parts, axis=1)
    up_parts = jnp.concatenate([up_block] * 3, axis=1)
    return jnp.einsum("nrb,nro->nbo", parts, up_parts, preferred_element_type=jnp.float32)


def body(tokens, base_weight, down_tables, up_tables, block_owner, block_local, block_count):
    tp_count = lax.axis_size("tp")
    z = lax.axis_index("tp")
    width = base_weight.shape[1] // tp_count
    owners = block_owner[:, 0]

    def product(block):
        columns = lax.dynamic_slice_in_dim(base_weight, block * width, width, 1)
        value = jnp.dot(tokens, columns, preferred_element_type=jnp.float32)
        return with_layout_constraint(value, Layout((0, 1)))

    scale = 2.0 ** math.floor(math.log2(FLOAT16_MAX / (2 * tokens.shape[1] * PRODUCT_MAX)))

    def code(value):
        return (value * scale).astype(jnp.float16)

    def plain(value):
        return value.astype(jnp.float32) * (1.0 / scale)

    def after(value, *others):
        return lax.optimization_barrier((value, *others))[0]

    id_steps = list(adapter_ids(block_owner, block_local, down_tables.shape[0]))
    live_counts = block_count
    if tp_count == 4:
        end = (z == 0) | (z == 3)
        far = after(code(product(z ^ 3)), id_steps[0])
        to_inner = lax.ppermute(far, "tp", [(0, 1), (3, 2)])
        direct, z = lax.optimization_barrier((far, z))
        from_inner = lax.ppermute(direct, "tp", [(1, 2), (2, 1)])
        later_z = after(z, id_steps[1])
        first = code(product(later_z ^ jnp.where(end, 2, 1)))
        from_first = lax.ppermute(first, "tp", [(0, 2), (3, 1), (1, 0), (2, 3)])
        packed = pack_adapters(after(id_steps[-1], first), down_tables, up_tables)
        later_z, packed = lax.optimization_barrier((z, packed))
        got = exchange(packed)
        second = product(later_z ^ jnp.where(end, 1, 2))
        second = code(second + plain(to_inner))
        from_second = lax.ppermute(second, "tp", [(0, 1), (3, 2), (1, 3), (2, 0)])
        own = lax.optimization_barrier(product(after(z, second)))
        live_counts = after(block_count, own)
        base_projection = lax.optimization_barrier(own + plain(from_first))
        block_slot = slot_plan(later(owners, base_projection))
        reduced, up_block = reduce_tokens(tokens, got, block_slot)
        from_second = after(from_second, reduced)
        base_projection = lax.optimization_barrier(base_projection + plain(from_inner) + plain(from_second))
    else:
        partial_value = jnp.dot(tokens, base_weight, preferred_element_type=jnp.float32)
        base_projection = lax.psum_scatter(partial_value, "tp", scatter_dimension=1, tiled=True)
        got = exchange(pack_adapters(id_steps[-1], down_tables, up_tables))
        reduced, up_block = reduce_tokens(tokens, got, slot_plan(owners))
    total = reduced
    for j in range(1, tp_count):
        total = total + lax.ppermute(reduced, "tp", [(i, i ^ j) for i in range(tp_count)])
    lowrank = expand_tokens(total, up_block)
    offsets = jnp.arange(BLOCK, dtype=jnp.int32)
    live_rows = offsets[None, :, None] < live_counts[:, None, None]
    combined_output = base_projection.reshape(lowrank.shape) + adapter_scale * lowrank
    projected = jnp.where(live_rows, combined_output, jnp.float32(0.0)).astype(jnp.bfloat16)
    return projected.reshape(base_projection.shape)


def solution(mesh):
    placed = (
        P("grp", "tp"),
        P("tp", None),
        P("grp", "tp", None),
        P("grp", None, "tp"),
        P("grp", None),
        P("grp"),
        P("grp"),
    )
    return jax.shard_map(body, mesh=mesh, in_specs=placed, out_specs=P("grp", "tp"), check_vma=False)
```

```python
import math

import jax
import jax.numpy as jnp
from jax import lax
from jax.experimental import pallas as pl
from jax.experimental.pallas import tpu as pltpu
from jax.experimental.layout import Layout, with_layout_constraint
from jax.sharding import PartitionSpec as P

BLOCK = 128
CAP = 2
adapter_scale = 2.0
FLOAT16_MAX = 65504.0
PRODUCT_MAX = 6.0 * 0.0625
HBM = pl.BlockSpec(memory_space=pl.ANY)


def pack_kernel(ids_ref, me_ref, down_ref, up_ref, out_ref, held, read_sems, write_sem):
    groups, blocks = ids_ref.shape
    local_total, _, cols = down_ref.shape
    low = me_ref[0] * local_total
    wanted = []
    for j in range(groups):
        slots, seen = [jnp.int32(0)] * CAP, jnp.int32(0)
        for b in range(blocks):
            local = ids_ref[j, b] - low
            mine = (local >= 0) & (local < local_total)
            slots = [jnp.where(mine & (seen == r), local, s) for r, s in enumerate(slots)]
            seen = seen + mine.astype(jnp.int32)
        for r, slot in enumerate(slots):
            k = j * CAP + r
            reads = [
                pltpu.make_async_copy(down_ref.at[slot], held.at[k, :, pl.ds(0, cols)], read_sems.at[k]),
                pltpu.make_async_copy(up_ref.at[slot], held.at[k, :, pl.ds(cols, up_ref.shape[2])], read_sems.at[k]),
            ]
            write = pltpu.make_async_copy(held.at[k], out_ref.at[me_ref[0] ^ j, r], write_sem)
            wanted.append((seen > r, reads, write))

            @pl.when(seen > r)
            def _():
                reads[0].start()
                reads[1].start()

    for there, reads, write in wanted:

        @pl.when(there)
        def _():
            reads[0].wait()
            reads[1].wait()
            write.start()

    for there, reads, write in wanted:

        @pl.when(there)
        def _():
            write.wait()


def later_kernel(value_ref, out_ref, sem):
    copy = pltpu.make_async_copy(value_ref, out_ref, sem)
    copy.start()
    copy.wait()


LONG = pl.CostEstimate(flops=100_000_000_000, bytes_accessed=1, transcendentals=0)
CHEAP = pl.CostEstimate(flops=1, bytes_accessed=1, transcendentals=0)


def adapter_ids(block_owner, block_local, local_total):
    group_count = lax.axis_size("grp")
    ids = (block_owner[:, 0] * local_total + block_local).reshape(1, block_owner.shape[0])
    step = 1
    while step < group_count:
        there = lax.ppermute(ids, "grp", [(i, i ^ step) for i in range(group_count)])
        ids = jnp.concatenate([ids, there], axis=0)
        yield ids
        step *= 2


def pack_adapters(ids, down_tables, up_tables):
    group_count = lax.axis_size("grp")
    me = lax.axis_index("grp").astype(jnp.int32).reshape(1)
    _, cols, rank = down_tables.shape
    wide = cols + up_tables.shape[2]
    return pl.pallas_call(
        pack_kernel,
        out_shape=jax.ShapeDtypeStruct((group_count, CAP, rank, wide), jnp.bfloat16),
        grid_spec=pltpu.PrefetchScalarGridSpec(
            num_scalar_prefetch=2,
            in_specs=[HBM, HBM],
            out_specs=HBM,
            scratch_shapes=[
                pltpu.VMEM((group_count * CAP, rank, wide), jnp.bfloat16),
                pltpu.SemaphoreType.DMA((group_count * CAP,)),
                pltpu.SemaphoreType.DMA,
            ],
        ),
        cost_estimate=CHEAP,
    )(ids, me, jnp.transpose(down_tables, (0, 2, 1)), up_tables)


def exchange(packed):
    got = lax.all_to_all(packed, "grp", split_axis=0, concat_axis=0, tiled=True)
    return got.reshape(got.shape[0] * CAP, *got.shape[2:])


def later(value, *others):
    value = lax.optimization_barrier((value, *others))[0]
    return pl.pallas_call(
        later_kernel,
        out_shape=jax.ShapeDtypeStruct(value.shape, value.dtype),
        in_specs=[HBM],
        out_specs=HBM,
        scratch_shapes=[pltpu.SemaphoreType.DMA],
        cost_estimate=LONG,
    )(value)


def slot_plan(owners):
    order = jnp.arange(owners.shape[0], dtype=jnp.int32)
    earlier = (owners[None, :] == owners[:, None]) & (order[None, :] < order[:, None])
    return owners * CAP + jnp.sum(earlier.astype(jnp.int32), axis=1)


def reduce_tokens(tokens, got, block_slot):
    blocks, cols = block_slot.shape[0], tokens.shape[1]
    match = block_slot[:, None] == jnp.arange(got.shape[0], dtype=jnp.int32)[None, :]
    mine = jnp.sum(jnp.where(match[:, :, None, None], got[None], jnp.bfloat16(0.0)).astype(jnp.float32), axis=1).astype(jnp.bfloat16)
    mine = lax.optimization_barrier(mine)
    down_block = lax.optimization_barrier(mine[:, :, :cols])
    blocked = tokens.reshape(blocks, BLOCK, cols)
    reduced = jnp.einsum("nbd,nrd->nrb", blocked, down_block, preferred_element_type=jnp.float32)
    up_block, _ = lax.optimization_barrier((mine[:, :, cols:], reduced))
    return reduced, up_block


def expand_tokens(total, up_block):
    parts, rest = [], total
    for _ in range(3):
        part = lax.reduce_precision(rest, exponent_bits=8, mantissa_bits=7)
        parts.append(part.astype(jnp.bfloat16))
        rest = rest - part
    parts = jnp.concatenate(parts, axis=1)
    up_parts = jnp.concatenate([up_block] * 3, axis=1)
    return jnp.einsum("nrb,nro->nbo", parts, up_parts, preferred_element_type=jnp.float32)


def body(tokens, base_weight, down_tables, up_tables, block_owner, block_local, block_count):
    tp_count = lax.axis_size("tp")
    z = lax.axis_index("tp")
    width = base_weight.shape[1] // tp_count
    owners = block_owner[:, 0]

    def product(block):
        columns = lax.dynamic_slice_in_dim(base_weight, block * width, width, 1)
        value = jnp.dot(tokens, columns, preferred_element_type=jnp.float32)
        return with_layout_constraint(value, Layout((0, 1)))

    scale = 2.0 ** math.floor(math.log2(FLOAT16_MAX / (2 * tokens.shape[1] * PRODUCT_MAX)))

    def code(value):
        return (value * scale).astype(jnp.float16)

    def plain(value):
        return value.astype(jnp.float32) * (1.0 / scale)

    def after(value, *others):
        return lax.optimization_barrier((value, *others))[0]

    id_steps = list(adapter_ids(block_owner, block_local, down_tables.shape[0]))
    live_counts = block_count
    if tp_count == 4:
        end = (z == 0) | (z == 3)
        far = after(code(product(z ^ 3)), id_steps[0])
        to_inner = lax.ppermute(far, "tp", [(0, 1), (3, 2)])
        direct, z = lax.optimization_barrier((far, z))
        from_inner = lax.ppermute(direct, "tp", [(1, 2), (2, 1)])
        later_z = after(z, id_steps[1])
        first = code(product(later_z ^ jnp.where(end, 2, 1)))
        from_first = lax.ppermute(first, "tp", [(0, 2), (3, 1), (1, 0), (2, 3)])
        packed = pack_adapters(after(id_steps[-1], first), down_tables, up_tables)
        later_z, packed = lax.optimization_barrier((z, packed))
        got = exchange(packed)
        second = product(later_z ^ jnp.where(end, 1, 2))
        second = code(second + plain(to_inner))
        from_second = lax.ppermute(second, "tp", [(0, 1), (3, 2), (1, 3), (2, 0)])
        own = lax.optimization_barrier(product(after(z, second)))
        live_counts = after(block_count, own)
        base_projection = lax.optimization_barrier(own + plain(from_first))
        block_slot = slot_plan(later(owners, own))
        reduced, up_block = reduce_tokens(tokens, got, block_slot)
        from_second = after(from_second, reduced)
        base_projection = lax.optimization_barrier(base_projection + plain(from_inner) + plain(from_second))
    else:
        partial_value = jnp.dot(tokens, base_weight, preferred_element_type=jnp.float32)
        base_projection = lax.psum_scatter(partial_value, "tp", scatter_dimension=1, tiled=True)
        got = exchange(pack_adapters(id_steps[-1], down_tables, up_tables))
        reduced, up_block = reduce_tokens(tokens, got, slot_plan(owners))
    total = reduced
    for j in range(1, tp_count):
        total = total + lax.ppermute(reduced, "tp", [(i, i ^ j) for i in range(tp_count)])
    lowrank = expand_tokens(total, up_block)
    offsets = jnp.arange(BLOCK, dtype=jnp.int32)
    live_rows = offsets[None, :, None] < live_counts[:, None, None]
    combined_output = base_projection.reshape(lowrank.shape) + adapter_scale * lowrank
    projected = jnp.where(live_rows, combined_output, jnp.float32(0.0)).astype(jnp.bfloat16)
    return projected.reshape(base_projection.shape)


def solution(mesh):
    placed = (
        P("grp", "tp"),
        P("tp", None),
        P("grp", "tp", None),
        P("grp", None, "tp"),
        P("grp", None),
        P("grp"),
        P("grp"),
    )
    return jax.shard_map(body, mesh=mesh, in_specs=placed, out_specs=P("grp", "tp"), check_vma=False)
```

```python
import math

import jax
import jax.numpy as jnp
from jax import lax
from jax.experimental import pallas as pl
from jax.experimental.pallas import tpu as pltpu
from jax.experimental.layout import Layout, with_layout_constraint
from jax.sharding import PartitionSpec as P

BLOCK = 128
CAP = 2
adapter_scale = 2.0
FLOAT16_MAX = 65504.0
PRODUCT_MAX = 6.0 * 0.0625
HBM = pl.BlockSpec(memory_space=pl.ANY)


def pack_kernel(ids_ref, me_ref, down_ref, up_ref, out_ref, held, read_sems, write_sem):
    groups, blocks = ids_ref.shape
    local_total, _, cols = down_ref.shape
    low = me_ref[0] * local_total
    wanted = []
    for j in range(groups):
        slots, seen = [jnp.int32(0)] * CAP, jnp.int32(0)
        for b in range(blocks):
            local = ids_ref[j, b] - low
            mine = (local >= 0) & (local < local_total)
            slots = [jnp.where(mine & (seen == r), local, s) for r, s in enumerate(slots)]
            seen = seen + mine.astype(jnp.int32)
        for r, slot in enumerate(slots):
            k = j * CAP + r
            reads = [
                pltpu.make_async_copy(down_ref.at[slot], held.at[k, :, pl.ds(0, cols)], read_sems.at[k]),
                pltpu.make_async_copy(up_ref.at[slot], held.at[k, :, pl.ds(cols, up_ref.shape[2])], read_sems.at[k]),
            ]
            write = pltpu.make_async_copy(held.at[k], out_ref.at[me_ref[0] ^ j, r], write_sem)
            wanted.append((seen > r, reads, write))

            @pl.when(seen > r)
            def _():
                reads[0].start()
                reads[1].start()

    for there, reads, write in wanted:

        @pl.when(there)
        def _():
            reads[0].wait()
            reads[1].wait()
            write.start()

    for there, reads, write in wanted:

        @pl.when(there)
        def _():
            write.wait()


def later_kernel(value_ref, out_ref, sem):
    copy = pltpu.make_async_copy(value_ref, out_ref, sem)
    copy.start()
    copy.wait()


LONG = pl.CostEstimate(flops=100_000_000_000, bytes_accessed=1, transcendentals=0)
CHEAP = pl.CostEstimate(flops=1, bytes_accessed=1, transcendentals=0)


def adapter_ids(block_owner, block_local, local_total):
    group_count = lax.axis_size("grp")
    ids = (block_owner[:, 0] * local_total + block_local).reshape(1, block_owner.shape[0])
    step = 1
    while step < group_count:
        there = lax.ppermute(ids, "grp", [(i, i ^ step) for i in range(group_count)])
        ids = jnp.concatenate([ids, there], axis=0)
        yield ids
        step *= 2


def pack_adapters(ids, down_tables, up_tables):
    group_count = lax.axis_size("grp")
    me = lax.axis_index("grp").astype(jnp.int32).reshape(1)
    _, cols, rank = down_tables.shape
    wide = cols + up_tables.shape[2]
    return pl.pallas_call(
        pack_kernel,
        out_shape=jax.ShapeDtypeStruct((group_count, CAP, rank, wide), jnp.bfloat16),
        grid_spec=pltpu.PrefetchScalarGridSpec(
            num_scalar_prefetch=2,
            in_specs=[HBM, HBM],
            out_specs=HBM,
            scratch_shapes=[
                pltpu.VMEM((group_count * CAP, rank, wide), jnp.bfloat16),
                pltpu.SemaphoreType.DMA((group_count * CAP,)),
                pltpu.SemaphoreType.DMA,
            ],
        ),
        cost_estimate=CHEAP,
    )(ids, me, jnp.transpose(down_tables, (0, 2, 1)), up_tables)


def exchange(packed):
    got = lax.all_to_all(packed, "grp", split_axis=0, concat_axis=0, tiled=True)
    return got.reshape(got.shape[0] * CAP, *got.shape[2:])


def later(value, *others):
    value = lax.optimization_barrier((value, *others))[0]
    return pl.pallas_call(
        later_kernel,
        out_shape=jax.ShapeDtypeStruct(value.shape, value.dtype),
        in_specs=[HBM],
        out_specs=HBM,
        scratch_shapes=[pltpu.SemaphoreType.DMA],
        cost_estimate=LONG,
    )(value)


def slot_plan(owners):
    order = jnp.arange(owners.shape[0], dtype=jnp.int32)
    earlier = (owners[None, :] == owners[:, None]) & (order[None, :] < order[:, None])
    return owners * CAP + jnp.sum(earlier.astype(jnp.int32), axis=1)


def reduce_tokens(tokens, got, block_slot):
    blocks, cols = block_slot.shape[0], tokens.shape[1]
    match = block_slot[:, None] == jnp.arange(got.shape[0], dtype=jnp.int32)[None, :]
    mine = jnp.sum(jnp.where(match[:, :, None, None], got[None], jnp.bfloat16(0.0)).astype(jnp.float32), axis=1).astype(jnp.bfloat16)
    down_block = mine[:, :, :cols]
    blocked = tokens.reshape(blocks, BLOCK, cols)
    reduced = jnp.einsum("nbd,nrd->nrb", blocked, down_block, preferred_element_type=jnp.float32)
    up_block, _ = lax.optimization_barrier((mine[:, :, cols:], reduced))
    return reduced, up_block


def expand_tokens(total, up_block):
    parts, rest = [], total
    for _ in range(3):
        part = lax.reduce_precision(rest, exponent_bits=8, mantissa_bits=7)
        parts.append(part.astype(jnp.bfloat16))
        rest = rest - part
    parts = jnp.concatenate(parts, axis=1)
    up_parts = jnp.concatenate([up_block] * 3, axis=1)
    return jnp.einsum("nrb,nro->nbo", parts, up_parts, preferred_element_type=jnp.float32)


def body(tokens, base_weight, down_tables, up_tables, block_owner, block_local, block_count):
    tp_count = lax.axis_size("tp")
    z = lax.axis_index("tp")
    width = base_weight.shape[1] // tp_count
    owners = block_owner[:, 0]

    def product(block):
        columns = lax.dynamic_slice_in_dim(base_weight, block * width, width, 1)
        value = jnp.dot(tokens, columns, preferred_element_type=jnp.float32)
        return with_layout_constraint(value, Layout((0, 1)))

    scale = 2.0 ** math.floor(math.log2(FLOAT16_MAX / (2 * tokens.shape[1] * PRODUCT_MAX)))

    def code(value):
        return (value * scale).astype(jnp.float16)

    def plain(value):
        return value.astype(jnp.float32) * (1.0 / scale)

    def after(value, *others):
        return lax.optimization_barrier((value, *others))[0]

    id_steps = list(adapter_ids(block_owner, block_local, down_tables.shape[0]))
    live_counts = block_count
    if tp_count == 4:
        end = (z == 0) | (z == 3)
        far = after(code(product(z ^ 3)), id_steps[0])
        to_inner = lax.ppermute(far, "tp", [(0, 1), (3, 2)])
        direct, z = lax.optimization_barrier((far, z))
        from_inner = lax.ppermute(direct, "tp", [(1, 2), (2, 1)])
        later_z = after(z, id_steps[1])
        first = code(product(later_z ^ jnp.where(end, 2, 1)))
        from_first = lax.ppermute(first, "tp", [(0, 2), (3, 1), (1, 0), (2, 3)])
        packed = pack_adapters(after(id_steps[-1], first), down_tables, up_tables)
        later_z, packed = lax.optimization_barrier((z, packed))
        got = exchange(packed)
        second = product(later_z ^ jnp.where(end, 1, 2))
        second = code(second + plain(to_inner))
        from_second = lax.ppermute(second, "tp", [(0, 1), (3, 2), (1, 3), (2, 0)])
        own = lax.optimization_barrier(product(after(z, second)))
        live_counts = after(block_count, own)
        base_projection = lax.optimization_barrier(own + plain(from_first))
        block_slot = slot_plan(later(owners, base_projection))
        reduced, up_block = reduce_tokens(tokens, got, block_slot)
        from_second = after(from_second, reduced)
        base_projection = lax.optimization_barrier(base_projection + plain(from_inner) + plain(from_second))
    else:
        partial_value = jnp.dot(tokens, base_weight, preferred_element_type=jnp.float32)
        base_projection = lax.psum_scatter(partial_value, "tp", scatter_dimension=1, tiled=True)
        got = exchange(pack_adapters(id_steps[-1], down_tables, up_tables))
        reduced, up_block = reduce_tokens(tokens, got, slot_plan(owners))
    total = reduced
    for j in range(1, tp_count):
        total = total + lax.ppermute(reduced, "tp", [(i, i ^ j) for i in range(tp_count)])
    lowrank = expand_tokens(total, up_block)
    offsets = jnp.arange(BLOCK, dtype=jnp.int32)
    live_rows = offsets[None, :, None] < live_counts[:, None, None]
    combined_output = base_projection.reshape(lowrank.shape) + adapter_scale * lowrank
    projected = jnp.where(live_rows, combined_output, jnp.float32(0.0)).astype(jnp.bfloat16)
    return projected.reshape(base_projection.shape)


def solution(mesh):
    placed = (
        P("grp", "tp"),
        P("tp", None),
        P("grp", "tp", None),
        P("grp", None, "tp"),
        P("grp", None),
        P("grp"),
        P("grp"),
    )
    return jax.shard_map(body, mesh=mesh, in_specs=placed, out_specs=P("grp", "tp"), check_vma=False)
```
